512 devices in a mesh: half: 2 (over core), grp: 256 (over x, y, z).
Axes of the slice: x: 4, y: 4, z: 16, core: 2. Of those that a mesh axis runs over, the one named last changes fastest.
Arguments:
- images: bfloat16 [131072, 2048], P(('half', 'grp')), parts along dimension 0, may hold values from -6 to 6
- projection: bfloat16 [4096, 256], replicated, may hold values from -0.375 to 0.375
- volume: bfloat16 [512, 2048], P(('half', 'grp')), parts along dimension 0, may hold values from -6 to 6
- subset: int32 [512, 1024], P(('half', 'grp')), parts along dimension 0, may hold values from 0 to 4095, all different within a row
- precision: float32 [131072], P(('half', 'grp')), parts along dimension 0, may hold values from 0.005 to 0.3
Outputs:
- new_volume: float32 [512, 2048], P(('half', 'grp')), parts along dimension 0
- log_evidence: float32 [131072], P(('half', 'grp')), parts along dimension 0
The draws below stay inside these ranges and needn't reach their ends.
There are 2 independent parts, one for each index of `half`. The reference program is written for one: setup_inputs(seed, part) draws one part's arguments, and reference() takes and returns one part's arrays. A program takes and returns all parts, laid end to end along the dimension named above; an argument that names none is the same for every part. Nothing has to cross between parts.
Inputs may be any that keep to these rules, and one draw needn't show every extreme that they name: `subset`: each row holds 1024 different orientations, and every orientation is searched by some block.
All inputs are finite; a program needn't handle non-finite values.
Results may differ from the reference program's by a relative error of at most 0.025.
Values may be sent and summed in bfloat16 or wider, within the bound.
No kernel may reach another device: no remote copies, remote signals or barrier semaphores. Data moves between devices by JAX's collectives and lax.ppermute only.
A program may use at most 64 MiB of HBM per device.

```python
import math
import jax
import jax.numpy as jnp
from jax import lax

BOX = 256
FREQ = 2048
ORI = 4096
SUB = 1024
PARTICLES = 65536
N_GRP = 256


def levels(key, dims, split, low, largest):
    def one(position, shards_of):
        draws = jax.random.uniform(jax.random.fold_in(jax.random.fold_in(key, 6), position), (shards_of,), jnp.float32, low / len(split), largest / len(split))
        return jnp.repeat(jnp.exp(draws), dims[position] // shards_of).reshape((-1,) + (1,) * (len(dims) - position - 1))

    factor_of = one(*split[0])
    for cut in split[1:]:
        factor_of = factor_of * one(*cut)
    return factor_of


def choose_distinct(own_key, rows, count, top, lift):
    ranking = jax.random.permutation(jax.random.fold_in(own_key, 1), count)
    pull = ranking
    for power in range(3):
        pull = pull * pull // count
    pull = pull * lift // count
    chance = jax.random.randint(jax.random.fold_in(own_key, 2), (rows, count), 0, 4096) + pull
    fixed_rows = jax.random.permutation(jax.random.fold_in(own_key, 3), rows)[jnp.arange(count) % rows]
    chance = jnp.where(jnp.arange(rows)[:, None] == fixed_rows[None, :], 1 << 14, chance)
    score = chance * count + jnp.arange(count)
    return lax.top_k(score.astype(jnp.int32), top)[1].astype(jnp.int32)


def scatter_about(key, dims, spread, limit, pieces=(), dtype=jnp.bfloat16):
    result = spread * jax.random.normal(key, dims, jnp.float32)
    if pieces:
        result = result * levels(key, dims, pieces, -0.22, 0.18)
    return jnp.clip(result, -limit, limit).astype(dtype)


def setup_inputs(seed: int = 0, part: int = 0) -> dict:
    keys = jax.random.split(jax.random.key(seed), 6)
    own_keys = jax.random.split(jax.random.fold_in(keys[5], part), 6)
    images = scatter_about(own_keys[0], (PARTICLES, FREQ), 1.0, 6.0, ((0, 256),))
    projection = scatter_about(keys[1], (ORI, BOX), BOX ** -0.5, 0.375)
    volume = scatter_about(own_keys[2], (BOX, FREQ), 1.0, 6.0, ((0, 256),))
    subset = choose_distinct(own_keys[3], N_GRP, ORI, SUB, 0)
    precision = jnp.clip(jnp.exp(math.log(0.3) - 4.0943446 * jax.random.uniform(own_keys[4], (PARTICLES,), jnp.float32) ** levels(own_keys[4], (PARTICLES,), ((0, 256),), -0.2, 0.2)), 0.005, 0.3)
    return {"images": images, "projection": projection, "volume": volume, "subset": subset, "precision": precision}


def one_block(images_block, picked, volume, precision_block):
    templates = jnp.dot(picked, volume, preferred_element_type=jnp.float32).astype(jnp.bfloat16)
    tfloat = templates.astype(jnp.float32)
    energy = jnp.sum(tfloat * tfloat, axis=1)
    corr = lax.dot_general(images_block, templates, (((1,), (1,)), ((), ())), preferred_element_type=jnp.float32)
    scores = precision_block[:, None] * (corr - 0.5 * energy[None, :])
    peak = jnp.max(scores, axis=1, keepdims=True)
    expo = jnp.exp(scores - peak)
    summed = jnp.sum(expo, axis=1, keepdims=True)
    evidence = peak + jnp.log(summed)
    weights = jnp.exp(scores - evidence)
    weights_low = weights.astype(jnp.bfloat16)
    backproj = lax.dot_general(weights_low, images_block, (((0,), (0,)), ((), ())), preferred_element_type=jnp.float32).astype(jnp.bfloat16)
    occupancy = jnp.sum(weights, axis=0)
    numer = lax.dot_general(picked, backproj, (((0,), (0,)), ((), ())), preferred_element_type=jnp.float32)
    pfloat = picked.astype(jnp.float32)
    slab_w = jnp.dot(occupancy, pfloat * pfloat, precision=lax.Precision.HIGHEST)
    return numer, slab_w, evidence[:, 0]


def reference(images, projection, volume, subset, precision):
    blocks = subset.shape[0]
    width = images.shape[1]
    img_blocks = images.reshape(blocks, -1, width)
    prec_blocks = precision.reshape(blocks, -1)

    def step(carry, inputs):
        numer_acc, weight_acc = carry
        img_b, sub_b, prec_b = inputs
        picked = jnp.take(projection, sub_b.astype(jnp.int32), axis=0)
        numer, slab_w, evidence = one_block(img_b, picked, volume, prec_b)
        return (numer_acc + numer, weight_acc + slab_w), evidence

    start = (jnp.zeros(volume.shape, jnp.float32), jnp.zeros((volume.shape[0],), jnp.float32))
    (numer_all, weight_all), evid = lax.scan(step, start, (img_blocks, subset, prec_blocks))
    new_volume = numer_all / (weight_all[:, None] + 1.0)
    return new_volume, evid.reshape(-1)
```

```python
import jax
import jax.numpy as jnp
from jax import lax
from jax.sharding import Mesh, PartitionSpec as P

X, Y, Z = 4, 4, 16
PLANE = ("x", "y")


def gather_slabs(volume):
    column = lax.all_to_all(
        jnp.broadcast_to(volume.reshape(1, 16, 128), (Z, 16, 128)), "z", 0, 0, tiled=True
    )
    column = column.reshape(Z, 2048)
    whole = lax.all_to_all(
        jnp.broadcast_to(column[None], (X * Y, Z, 2048)), PLANE, 0, 0, tiled=True
    )
    return whole.reshape(X * Y * Z, 2048)


def sum_slabs(partial):
    width = partial.shape[1]
    plane = lax.all_to_all(partial.reshape(X * Y, Z, width), PLANE, 0, 0, tiled=True)
    plane = jnp.sum(plane.astype(jnp.float32), axis=0).astype(jnp.bfloat16)
    column = lax.all_to_all(plane.reshape(Z, width // 128, 128), "z", 0, 0, tiled=True)
    return jnp.sum(column.astype(jnp.float32), axis=0).reshape(1, width)


def local(images, projection, volume, subset, precision):
    picked = jnp.take(projection, subset[0], axis=0)
    gathered = gather_slabs(volume)
    templ_full = jnp.dot(picked, gathered, preferred_element_type=jnp.float32)
    templates = templ_full.astype(jnp.bfloat16)
    tfloat = templates.astype(jnp.float32)
    energy = jnp.sum(tfloat * tfloat, axis=1)
    correlate = lax.dot_general(
        images, templates, (((1,), (1,)), ((), ())), preferred_element_type=jnp.float32
    )
    scores = precision[:, None] * (correlate - 0.5 * energy[None, :])
    highest = jnp.max(scores, axis=1, keepdims=True)
    summed = jnp.sum(jnp.exp(scores - highest), axis=1, keepdims=True)
    evidence = highest + jnp.log(summed)
    weights = jnp.exp(scores - evidence)
    weights_low = weights.astype(jnp.bfloat16)
    backproj = lax.dot_general(
        weights_low, images, (((0,), (0,)), ((), ())), preferred_element_type=jnp.float32
    ).astype(jnp.bfloat16)
    occupancy = jnp.sum(weights, axis=0)
    numerator = lax.dot_general(
        picked, backproj, (((0,), (0,)), ((), ())), preferred_element_type=jnp.float32
    )
    pfloat = picked.astype(jnp.float32)
    slab_weight = jnp.dot(occupancy, pfloat * pfloat, precision=lax.Precision.HIGHEST)
    high = slab_weight.astype(jnp.bfloat16)
    rest = (slab_weight - high.astype(jnp.float32)).astype(jnp.bfloat16)
    extra = jnp.concatenate(
        [high[:, None], rest[:, None], jnp.zeros((256, 126), jnp.bfloat16)], axis=1
    )
    mine = sum_slabs(jnp.concatenate([numerator.astype(jnp.bfloat16), extra], axis=1))
    weight_mine = mine[:, 2048:2049] + mine[:, 2049:2050]
    new_volume = mine[:, :2048] / (weight_mine + 1.0)
    return (new_volume, evidence[:, 0])


def solution(mesh):
    grid = Mesh(mesh.devices.reshape(2, X, Y, Z), ("half", "x", "y", "z"))
    every = ("half", "x", "y", "z")
    placed = (P(every, None), P(), P(every, None), P(every, None), P(every))
    return jax.shard_map(
        local,
        mesh=grid,
        in_specs=placed,
        out_specs=(P(every, None), P(every)),
        check_vma=False,
    )
```

```python
import jax
import jax.numpy as jnp
from jax import lax
from jax.experimental import pallas as pl
from jax.experimental.pallas import tpu as pltpu
from jax.sharding import Mesh, PartitionSpec as P

X, Y, Z = 4, 4, 16
PLANE = ("x", "y")
SLABS, FREQ, ORI, SUB, ROWS = 256, 2048, 4096, 1024, 256
WIDE = FREQ + 128
BF16, F32 = jnp.bfloat16, jnp.float32
NN = (((1,), (0,)), ((), ()))
NT = (((1,), (1,)), ((), ()))
TN = (((0,), (0,)), ((), ()))


def mm(a, b, dims):
    return lax.dot_general(a, b, dims, preferred_element_type=F32)


def parts(a, count):
    found = []
    for _ in range(count):
        found.append(a.astype(BF16))
        a = a - found[-1].astype(F32)
    return found


def pick_kernel(subset_ref, projection_ref, picked_ref, total_ref):
    subset = subset_ref[...]
    block = subset // 256
    within = subset - block * 256
    rows = lax.broadcasted_iota(jnp.int32, (256, SUB), 0).astype(F32).astype(BF16)
    for k in range(ORI // 256):
        wanted = jnp.where(block == k, within, -1).astype(F32).astype(BF16)
        chosen = jnp.where(rows == wanted, jnp.ones((), BF16), jnp.zeros((), BF16))
        part = mm(projection_ref[k * 256 : (k + 1) * 256, :], chosen, TN)
        if k == 0:
            total_ref[...] = part
        else:
            total_ref[...] += part
    picked_ref[...] = total_ref[...].astype(BF16)


def pick(subset, projection):
    return pl.pallas_call(
        pick_kernel,
        out_shape=jax.ShapeDtypeStruct((SLABS, SUB), BF16),
        in_specs=[pl.BlockSpec(memory_space=pltpu.VMEM)] * 2,
        out_specs=pl.BlockSpec(memory_space=pltpu.VMEM),
        scratch_shapes=[pltpu.VMEM((SLABS, SUB), F32)],
        compiler_params=pltpu.CompilerParams(vmem_limit_bytes=12 << 20),
        cost_estimate=pl.CostEstimate(
            flops=2 * SLABS * ORI * SUB, bytes_accessed=3 << 20, transcendentals=0
        ),
        name="pick_rows",
    )(subset, projection)


def expect_kernel(images_ref, volume_ref, picked_ref, precision_ref, partial_ref, evidence_ref):
    images, volume = images_ref[...], volume_ref[...]
    picked = picked_ref[...]
    gram = mm(volume, volume, NT)
    wide = sum(mm(g, picked, NN) for g in parts(gram, 3))
    pfloat = picked.astype(F32)
    energy = jnp.sum(wide * pfloat, axis=0, keepdims=True)
    cross = mm(images, volume, NT)
    correlate = sum(mm(c, picked, NN) for c in parts(cross, 3))
    precision = jnp.transpose(jnp.broadcast_to(precision_ref[...], (128, ROWS)))[:, :1]
    scores = precision * (correlate - 0.5 * energy)
    highest = jnp.max(scores, axis=1, keepdims=True)
    expo = jnp.exp(scores - highest)
    summed = jnp.sum(expo, axis=1, keepdims=True)
    evidence = highest + jnp.log(summed)
    evidence_ref[...] = jnp.transpose(jnp.broadcast_to(evidence, (ROWS, 128)))[:1, :]
    weights = expo * (1.0 / summed)
    occupancy = jnp.sum(weights, axis=0, keepdims=True)
    slab_weight = jnp.sum(occupancy * (pfloat * pfloat), axis=1, keepdims=True)
    mixed = mm(picked, weights.astype(BF16), NT).astype(BF16)
    for c in range(0, FREQ, 512):
        numer = mm(mixed, images_ref[:, c : c + 512], NN)
        partial_ref[:, :, c : c + 512] = numer.astype(BF16).reshape(X * Y, Z, 512)
    lane = lax.broadcasted_iota(jnp.int32, (SLABS, 128), 1)
    high = slab_weight.astype(BF16).astype(F32)
    extra = jnp.where(lane == 0, high, jnp.where(lane == 1, slab_weight - high, 0.0))
    partial_ref[:, :, FREQ:] = extra.astype(BF16).reshape(X * Y, Z, 128)


def expect(images, volume, picked, precision):
    return pl.pallas_call(
        expect_kernel,
        out_shape=(
            jax.ShapeDtypeStruct((X * Y, Z, WIDE), BF16),
            jax.ShapeDtypeStruct((1, ROWS), F32),
        ),
        in_specs=[pl.BlockSpec(memory_space=pltpu.VMEM)] * 4,
        out_specs=[pl.BlockSpec(memory_space=pltpu.VMEM)] * 2,
        compiler_params=pltpu.CompilerParams(vmem_limit_bytes=20 << 20),
        cost_estimate=pl.CostEstimate(
            flops=1400000000, bytes_accessed=4 << 20, transcendentals=ROWS * SUB
        ),
        name="expect",
    )(images, volume, picked, precision)


def gather_slabs(volume):
    column = lax.all_to_all(
        jnp.broadcast_to(volume.reshape(1, 16, 128), (Z, 16, 128)), "z", 0, 0, tiled=True
    )
    column = column.reshape(Z, FREQ)
    whole = lax.all_to_all(
        jnp.broadcast_to(column[None], (X * Y, Z, FREQ)), PLANE, 0, 0, tiled=True
    )
    return whole.reshape(SLABS, FREQ)


def sum_slabs(partial):
    plane = lax.all_to_all(partial, PLANE, 0, 0, tiled=True)
    plane = jnp.sum(plane.astype(F32), axis=0).astype(BF16)
    column = lax.all_to_all(plane.reshape(Z, WIDE // 128, 128), "z", 0, 0, tiled=True)
    return jnp.sum(column.astype(F32), axis=0).reshape(1, WIDE)


def local(images, projection, volume, subset, precision):
    gathered = gather_slabs(volume)
    picked = pick(subset, projection)
    partial, evidence = expect(images, gathered, picked, precision.reshape(1, ROWS))
    mine = sum_slabs(partial)
    weight_mine = mine[:, FREQ : FREQ + 1] + mine[:, FREQ + 1 : FREQ + 2]
    return (mine[:, :FREQ] / (weight_mine + 1.0), evidence.reshape(ROWS))


def solution(mesh):
    grid = Mesh(mesh.devices.reshape(2, X, Y, Z), ("half", "x", "y", "z"))
    every = ("half", "x", "y", "z")
    placed = (P(every, None), P(), P(every, None), P(every, None), P(every))
    return jax.shard_map(
        local,
        mesh=grid,
        in_specs=placed,
        out_specs=(P(every, None), P(every)),
        check_vma=False,
    )
```

```python
import jax
import jax.numpy as jnp
from jax import lax
from jax.experimental import pallas as pl
from jax.experimental.pallas import tpu as pltpu
from jax.sharding import Mesh, PartitionSpec as P

X, Y, Z = 4, 4, 16
PLANE = ("x", "y")
SLABS, FREQ, ORI, SUB, ROWS = 256, 2048, 4096, 1024, 256
WIDE = FREQ + 128
BF16, F32 = jnp.bfloat16, jnp.float32
NN = (((1,), (0,)), ((), ()))
NT = (((1,), (1,)), ((), ()))
TN = (((0,), (0,)), ((), ()))


def mm(a, b, dims):
    return lax.dot_general(a, b, dims, preferred_element_type=F32)


def parts(a, count):
    found = []
    for _ in range(count):
        found.append(a.astype(BF16))
        a = a - found[-1].astype(F32)
    return found


def pick_kernel(subset_ref, projection_ref, picked_ref, total_ref):
    subset = subset_ref[...]
    block = subset // 256
    within = subset - block * 256
    rows = lax.broadcasted_iota(jnp.int32, (256, SUB), 0).astype(F32).astype(BF16)
    for k in range(ORI // 256):
        wanted = jnp.where(block == k, within, -1).astype(F32).astype(BF16)
        chosen = jnp.where(rows == wanted, jnp.ones((), BF16), jnp.zeros((), BF16))
        part = mm(projection_ref[k * 256 : (k + 1) * 256, :], chosen, TN)
        if k == 0:
            total_ref[...] = part
        else:
            total_ref[...] += part
    picked_ref[...] = total_ref[...].astype(BF16)


def pick(subset, projection):
    return pl.pallas_call(
        pick_kernel,
        out_shape=jax.ShapeDtypeStruct((SLABS, SUB), BF16),
        in_specs=[pl.BlockSpec(memory_space=pltpu.VMEM)] * 2,
        out_specs=pl.BlockSpec(memory_space=pltpu.VMEM),
        scratch_shapes=[pltpu.VMEM((SLABS, SUB), F32)],
        compiler_params=pltpu.CompilerParams(vmem_limit_bytes=12 << 20),
        cost_estimate=pl.CostEstimate(
            flops=2 * SLABS * ORI * SUB, bytes_accessed=3 << 20, transcendentals=0
        ),
        name="pick_rows",
    )(subset, projection)


def expect_kernel(images_ref, volume_ref, picked_ref, precision_ref, partial_ref, evidence_ref):
    images, volume = images_ref[...], volume_ref[...]
    picked = picked_ref[...]
    gram = mm(volume, volume, NT)
    wide = sum(mm(g, picked, NN) for g in parts(gram, 3))
    pfloat = picked.astype(F32)
    energy = jnp.sum(wide * pfloat, axis=0, keepdims=True)
    cross = mm(images, volume, NT)
    correlate = sum(mm(c, picked, NN) for c in parts(cross, 3))
    precision = jnp.transpose(jnp.broadcast_to(precision_ref[...], (128, ROWS)))[:, :1]
    scores = precision * (correlate - 0.5 * energy)
    highest = jnp.max(scores, axis=1, keepdims=True)
    expo = jnp.exp(scores - highest)
    summed = jnp.sum(expo, axis=1, keepdims=True)
    evidence = highest + jnp.log(summed)
    evidence_ref[...] = jnp.transpose(jnp.broadcast_to(evidence, (ROWS, 128)))[:1, :]
    weights = expo * (1.0 / summed)
    occupancy = jnp.sum(weights, axis=0, keepdims=True)
    slab_weight = jnp.sum(occupancy * (pfloat * pfloat), axis=1, keepdims=True)
    mixed = mm(picked, weights.astype(BF16), NT).astype(BF16)
    for c in range(0, FREQ, 512):
        numer = mm(mixed, images_ref[:, c : c + 512], NN)
        partial_ref[:, :, c : c + 512] = numer.astype(BF16).reshape(X * Y, Z, 512)
    lane = lax.broadcasted_iota(jnp.int32, (SLABS, 128), 1)
    high = slab_weight.astype(BF16).astype(F32)
    extra = jnp.where(lane == 0, high, jnp.where(lane == 1, slab_weight - high, 0.0))
    partial_ref[:, :, FREQ:] = extra.astype(BF16).reshape(X * Y, Z, 128)


def expect(images, volume, picked, precision):
    return pl.pallas_call(
        expect_kernel,
        out_shape=(
            jax.ShapeDtypeStruct((X * Y, Z, WIDE), BF16),
            jax.ShapeDtypeStruct((1, ROWS), F32),
        ),
        in_specs=[pl.BlockSpec(memory_space=pltpu.VMEM)] * 4,
        out_specs=[pl.BlockSpec(memory_space=pltpu.VMEM)] * 2,
        compiler_params=pltpu.CompilerParams(vmem_limit_bytes=20 << 20),
        cost_estimate=pl.CostEstimate(
            flops=1400000000, bytes_accessed=4 << 20, transcendentals=ROWS * SUB
        ),
        name="expect",
    )(images, volume, picked, precision)


def gather_slabs(volume, picked):
    column = lax.all_to_all(
        jnp.broadcast_to(volume.reshape(1, 16, 128), (Z, 16, 128)), "z", 0, 0, tiled=True
    )
    column, picked = lax.optimization_barrier((column.reshape(Z, FREQ), picked))
    whole = lax.all_to_all(
        jnp.broadcast_to(column[None], (X * Y, Z, FREQ)), PLANE, 0, 0, tiled=True
    )
    return whole.reshape(SLABS, FREQ), picked


def finish_kernel(column_ref, new_ref):
    total = jnp.sum(column_ref[...].astype(F32), axis=0)
    weight = total[FREQ // 128 :, :1] + total[FREQ // 128 :, 1:2]
    new_ref[...] = total[: FREQ // 128, :] / (weight + 1.0)


def new_slab(partial):
    plane = lax.all_to_all(partial, PLANE, 0, 0, tiled=True)
    plane = jnp.sum(plane.astype(F32), axis=0).astype(BF16)
    column = lax.all_to_all(plane.reshape(Z, WIDE // 128, 128), "z", 0, 0, tiled=True)
    return pl.pallas_call(
        finish_kernel,
        out_shape=jax.ShapeDtypeStruct((FREQ // 128, 128), F32),
        in_specs=[pl.BlockSpec(memory_space=pltpu.VMEM)],
        out_specs=pl.BlockSpec(memory_space=pltpu.VMEM),
        compiler_params=pltpu.CompilerParams(vmem_limit_bytes=8 << 20),
        cost_estimate=pl.CostEstimate(flops=100000, bytes_accessed=1 << 17, transcendentals=0),
        name="finish",
    )(column).reshape(1, FREQ)


def local(images, projection, volume, subset, precision):
    gathered, picked = gather_slabs(volume, pick(subset, projection))
    partial, evidence = expect(images, gathered, picked, precision.reshape(1, ROWS))
    return (new_slab(partial), evidence.reshape(ROWS))


def solution(mesh):
    grid = Mesh(mesh.devices.reshape(2, X, Y, Z), ("half", "x", "y", "z"))
    every = ("half", "x", "y", "z")
    placed = (P(every, None), P(), P(every, None), P(every, None), P(every))
    return jax.shard_map(
        local,
        mesh=grid,
        in_specs=placed,
        out_specs=(P(every, None), P(every)),
        check_vma=False,
    )
```

```python
import jax
import jax.numpy as jnp
from jax import lax
from jax.experimental import pallas as pl
from jax.experimental.pallas import tpu as pltpu
from jax.sharding import Mesh, PartitionSpec as P

X, Y, Z = 4, 4, 16
PLANE = ("x", "y")
SLABS, FREQ, ORI, SUB, ROWS = 256, 2048, 4096, 1024, 256
WIDE = FREQ + 128
BF16, F32 = jnp.bfloat16, jnp.float32
NN = (((1,), (0,)), ((), ()))
NT = (((1,), (1,)), ((), ()))
TN = (((0,), (0,)), ((), ()))


def mm(a, b, dims):
    return lax.dot_general(a, b, dims, preferred_element_type=F32)


def parts(a, count):
    found = []
    for _ in range(count):
        found.append(a.astype(BF16))
        a = a - found[-1].astype(F32)
    return found


BLOCKS = 2
BLOCK = ORI // BLOCKS


def pick_rows(
    subset_hbm, projection_hbm, out_hbm, subset_ref, rows_ref, total_ref, picked_ref, sems
):
    subset_copy = pltpu.make_async_copy(subset_hbm, subset_ref, sems.at[BLOCKS])
    subset_copy.start()
    copies = []
    for b in range(BLOCKS):
        here = pl.ds(b * BLOCK, BLOCK)
        copies.append(
            pltpu.make_async_copy(projection_hbm.at[here], rows_ref.at[here], sems.at[b])
        )
        copies[-1].start()
    rows = lax.broadcasted_iota(jnp.int32, (256, SUB), 0).astype(F32).astype(BF16)
    subset_copy.wait()
    subset = subset_ref[...]
    block = subset // 256
    within = subset - block * 256
    for k in range(ORI // 256):
        wanted = jnp.where(block == k, within, -1).astype(F32).astype(BF16)
        chosen = jnp.where(rows == wanted, jnp.ones((), BF16), jnp.zeros((), BF16))
        if k * 256 % BLOCK == 0:
            copies[k * 256 // BLOCK].wait()
        part = mm(rows_ref[k * 256 : (k + 1) * 256, :], chosen, TN)
        if k == 0:
            total_ref[...] = part
        else:
            total_ref[...] += part
    picked_ref[...] = total_ref[...].astype(BF16)
    out = pltpu.make_async_copy(picked_ref, out_hbm, sems.at[BLOCKS])
    out.start()
    out.wait()


def pick_first_kernel(subset_hbm, projection_hbm, *refs):
    @pl.when(lax.axis_index("half") == 0)
    def _():
        pick_rows(subset_hbm, projection_hbm, *refs)


def pick_second_kernel(subset_hbm, projection_hbm, held_ref, *refs):
    @pl.when(lax.axis_index("half") == 1)
    def _():
        pick_rows(subset_hbm, projection_hbm, *refs)


def pick(kernel, name, subset, projection, *held):
    return pl.pallas_call(
        kernel,
        out_shape=jax.ShapeDtypeStruct((SLABS, SUB), BF16),
        in_specs=[pl.BlockSpec(memory_space=pltpu.HBM)] * (2 + len(held)),
        out_specs=pl.BlockSpec(memory_space=pltpu.HBM),
        input_output_aliases={2: 0} if held else {},
        scratch_shapes=[
            pltpu.VMEM((1, SUB), jnp.int32),
            pltpu.VMEM((ORI, SLABS), BF16),
            pltpu.VMEM((SLABS, SUB), F32),
            pltpu.VMEM((SLABS, SUB), BF16),
            pltpu.SemaphoreType.DMA((BLOCKS + 1,)),
        ],
        compiler_params=pltpu.CompilerParams(vmem_limit_bytes=60 << 20),
        cost_estimate=pl.CostEstimate(
            flops=2 * SLABS * ORI * SUB, bytes_accessed=3 << 20, transcendentals=0
        ),
        name=name,
    )(subset, projection, *held)


def expect_kernel(images_ref, volume_ref, picked_ref, precision_ref, partial_ref, evidence_ref):
    images, volume = images_ref[...], volume_ref[...]
    picked = picked_ref[...]
    gram = mm(volume, volume, NT)
    wide = sum(mm(g, picked, NN) for g in parts(gram, 3))
    pfloat = picked.astype(F32)
    energy = jnp.sum(wide * pfloat, axis=0, keepdims=True)
    cross = mm(images, volume, NT)
    correlate = sum(mm(c, picked, NN) for c in parts(cross, 3))
    precision = jnp.transpose(jnp.broadcast_to(precision_ref[...], (128, ROWS)))[:, :1]
    scores = precision * (correlate - 0.5 * energy)
    highest = jnp.max(scores, axis=1, keepdims=True)
    expo = jnp.exp(scores - highest)
    summed = jnp.sum(expo, axis=1, keepdims=True)
    evidence = highest + jnp.log(summed)
    evidence_ref[...] = jnp.transpose(jnp.broadcast_to(evidence, (ROWS, 128)))[:1, :]
    weights = expo * (1.0 / summed)
    occupancy = jnp.sum(weights, axis=0, keepdims=True)
    slab_weight = jnp.sum(occupancy * (pfloat * pfloat), axis=1, keepdims=True)
    mixed = mm(picked, weights.astype(BF16), NT).astype(BF16)
    for c in range(0, FREQ, 512):
        numer = mm(mixed, images_ref[:, c : c + 512], NN)
        partial_ref[:, :, c : c + 512] = numer.astype(BF16).reshape(X * Y, Z, 512)
    lane = lax.broadcasted_iota(jnp.int32, (SLABS, 128), 1)
    high = slab_weight.astype(BF16).astype(F32)
    extra = jnp.where(lane == 0, high, jnp.where(lane == 1, slab_weight - high, 0.0))
    partial_ref[:, :, FREQ:] = extra.astype(BF16).reshape(X * Y, Z, 128)


def expect(images, volume, picked, precision):
    return pl.pallas_call(
        expect_kernel,
        out_shape=(
            jax.ShapeDtypeStruct((X * Y, Z, WIDE), BF16),
            jax.ShapeDtypeStruct((1, ROWS), F32),
        ),
        in_specs=[pl.BlockSpec(memory_space=pltpu.VMEM)] * 4,
        out_specs=[pl.BlockSpec(memory_space=pltpu.VMEM)] * 2,
        compiler_params=pltpu.CompilerParams(vmem_limit_bytes=20 << 20),
        cost_estimate=pl.CostEstimate(
            flops=1400000000, bytes_accessed=4 << 20, transcendentals=ROWS * SUB
        ),
        name="expect",
    )(images, volume, picked, precision)


def gather_slabs(volume, subset, projection):
    picked = pick(pick_first_kernel, "pick_first", subset, projection)
    volume, picked = lax.optimization_barrier((volume, picked))
    column = lax.all_to_all(
        jnp.broadcast_to(volume.reshape(1, 16, 128), (Z, 16, 128)), "z", 0, 0, tiled=True
    )
    picked = pick(pick_second_kernel, "pick_second", subset, projection, picked)
    column, picked = lax.optimization_barrier((column.reshape(Z, FREQ), picked))
    whole = lax.all_to_all(
        jnp.broadcast_to(column[None], (X * Y, Z, FREQ)), PLANE, 0, 0, tiled=True
    )
    return whole.reshape(SLABS, FREQ), picked


def finish_kernel(column_ref, new_ref):
    total = jnp.sum(column_ref[...].astype(F32), axis=0)
    weight = total[FREQ // 128 :, :1] + total[FREQ // 128 :, 1:2]
    new_ref[...] = total[: FREQ // 128, :] / (weight + 1.0)


def new_slab(partial):
    plane = lax.all_to_all(partial, PLANE, 0, 0, tiled=True)
    plane = jnp.sum(plane.astype(F32), axis=0).astype(BF16)
    column = lax.all_to_all(plane.reshape(Z, WIDE // 128, 128), "z", 0, 0, tiled=True)
    return pl.pallas_call(
        finish_kernel,
        out_shape=jax.ShapeDtypeStruct((FREQ // 128, 128), F32),
        in_specs=[pl.BlockSpec(memory_space=pltpu.VMEM)],
        out_specs=pl.BlockSpec(memory_space=pltpu.VMEM),
        compiler_params=pltpu.CompilerParams(vmem_limit_bytes=8 << 20),
        cost_estimate=pl.CostEstimate(flops=100000, bytes_accessed=1 << 17, transcendentals=0),
        name="finish",
    )(column).reshape(1, FREQ)


def local(images, projection, volume, subset, precision):
    gathered, picked = gather_slabs(volume, subset, projection)
    partial, evidence = expect(images, gathered, picked, precision.reshape(1, ROWS))
    return (new_slab(partial), evidence.reshape(ROWS))


def solution(mesh):
    grid = Mesh(mesh.devices.reshape(2, X, Y, Z), ("half", "x", "y", "z"))
    every = ("half", "x", "y", "z")
    placed = (P(every, None), P(), P(every, None), P(every, None), P(every))
    return jax.shard_map(
        local,
        mesh=grid,
        in_specs=placed,
        out_specs=(P(every, None), P(every)),
        check_vma=False,
    )
```

```python
import jax
import jax.numpy as jnp
from jax import lax
from jax.experimental import pallas as pl
from jax.experimental.pallas import tpu as pltpu
from jax.sharding import Mesh, PartitionSpec as P

X, Y, Z = 4, 4, 16
PLANE = ("x", "y")
SLABS, FREQ, ORI, SUB, ROWS = 256, 2048, 4096, 1024, 256
WIDE = FREQ + 128
BF16, F32 = jnp.bfloat16, jnp.float32
NN = (((1,), (0,)), ((), ()))
NT = (((1,), (1,)), ((), ()))
TN = (((0,), (0,)), ((), ()))


def mm(a, b, dims):
    return lax.dot_general(a, b, dims, preferred_element_type=F32)


def parts(a, count):
    found = []
    for _ in range(count):
        found.append(a.astype(BF16))
        a = a - found[-1].astype(F32)
    return found


BLOCKS = 2
BLOCK = ORI // BLOCKS


def pick_rows(
    subset_hbm, projection_hbm, out_hbm, subset_ref, rows_ref, total_ref, picked_ref, sems
):
    subset_copy = pltpu.make_async_copy(subset_hbm, subset_ref, sems.at[BLOCKS])
    subset_copy.start()
    copies = []
    for b in range(BLOCKS):
        here = pl.ds(b * BLOCK, BLOCK)
        copies.append(
            pltpu.make_async_copy(projection_hbm.at[here], rows_ref.at[here], sems.at[b])
        )
        copies[-1].start()
    rows = lax.broadcasted_iota(jnp.int32, (256, SUB), 0).astype(F32).astype(BF16)
    subset_copy.wait()
    subset = subset_ref[...]
    block = subset // 256
    within = subset - block * 256
    for k in range(ORI // 256):
        wanted = jnp.where(block == k, within, -1).astype(F32).astype(BF16)
        chosen = jnp.where(rows == wanted, jnp.ones((), BF16), jnp.zeros((), BF16))
        if k * 256 % BLOCK == 0:
            copies[k * 256 // BLOCK].wait()
        part = mm(rows_ref[k * 256 : (k + 1) * 256, :], chosen, TN)
        if k == 0:
            total_ref[...] = part
        else:
            total_ref[...] += part
    picked_ref[...] = total_ref[...].astype(BF16)
    out = pltpu.make_async_copy(picked_ref, out_hbm, sems.at[BLOCKS])
    out.start()
    out.wait()


def pick_first_kernel(subset_hbm, projection_hbm, *refs):
    @pl.when(lax.axis_index("half") == 0)
    def _():
        pick_rows(subset_hbm, projection_hbm, *refs)


def pick_second_kernel(subset_hbm, projection_hbm, held_ref, *refs):
    @pl.when(lax.axis_index("half") == 1)
    def _():
        pick_rows(subset_hbm, projection_hbm, *refs)


def pick(kernel, name, subset, projection, *held):
    return pl.pallas_call(
        kernel,
        out_shape=jax.ShapeDtypeStruct((SLABS, SUB), BF16),
        in_specs=[pl.BlockSpec(memory_space=pltpu.HBM)] * (2 + len(held)),
        out_specs=pl.BlockSpec(memory_space=pltpu.HBM),
        input_output_aliases={2: 0} if held else {},
        scratch_shapes=[
            pltpu.VMEM((1, SUB), jnp.int32),
            pltpu.VMEM((ORI, SLABS), BF16),
            pltpu.VMEM((SLABS, SUB), F32),
            pltpu.VMEM((SLABS, SUB), BF16),
            pltpu.SemaphoreType.DMA((BLOCKS + 1,)),
        ],
        compiler_params=pltpu.CompilerParams(vmem_limit_bytes=60 << 20),
        cost_estimate=pl.CostEstimate(
            flops=2 * SLABS * ORI * SUB, bytes_accessed=3 << 20, transcendentals=0
        ),
        name=name,
    )(subset, projection, *held)


def expect_kernel(images_ref, volume_ref, picked_ref, precision_ref, partial_ref, evidence_ref):
    images, volume = images_ref[...], volume_ref[...]
    picked = picked_ref[...]
    gram = mm(volume, volume, NT)
    cross = mm(images, volume, NT)
    many = mm(jnp.concatenate(parts(gram, 3) + parts(cross, 3), axis=0), picked, NN)
    wide = sum(many[k * SLABS : (k + 1) * SLABS] for k in range(3))
    correlate = sum(many[k * ROWS : (k + 1) * ROWS] for k in range(3, 6))
    pfloat = picked.astype(F32)
    energy = jnp.sum(wide * pfloat, axis=0, keepdims=True)
    precision = jnp.transpose(jnp.broadcast_to(precision_ref[...], (128, ROWS)))[:, :1]
    scores = precision * (correlate - 0.5 * energy)
    highest = jnp.max(scores, axis=1, keepdims=True)
    expo = jnp.exp(scores - highest)
    summed = jnp.sum(expo, axis=1, keepdims=True)
    evidence = highest + jnp.log(summed)
    evidence_ref[...] = jnp.transpose(jnp.broadcast_to(evidence, (ROWS, 128)))[:1, :]
    weights = expo * (1.0 / summed)
    occupancy = jnp.sum(weights, axis=0, keepdims=True)
    slab_weight = jnp.sum(occupancy * (pfloat * pfloat), axis=1, keepdims=True)
    mixed = mm(picked, weights.astype(BF16), NT).astype(BF16)
    for c in range(0, FREQ, 512):
        numer = mm(mixed, images_ref[:, c : c + 512], NN)
        partial_ref[:, :, c : c + 512] = numer.astype(BF16).reshape(X * Y, Z, 512)
    lane = lax.broadcasted_iota(jnp.int32, (SLABS, 128), 1)
    high = slab_weight.astype(BF16).astype(F32)
    extra = jnp.where(lane == 0, high, jnp.where(lane == 1, slab_weight - high, 0.0))
    partial_ref[:, :, FREQ:] = extra.astype(BF16).reshape(X * Y, Z, 128)


def expect(images, volume, picked, precision):
    return pl.pallas_call(
        expect_kernel,
        out_shape=(
            jax.ShapeDtypeStruct((X * Y, Z, WIDE), BF16),
            jax.ShapeDtypeStruct((1, ROWS), F32),
        ),
        in_specs=[pl.BlockSpec(memory_space=pltpu.VMEM)] * 4,
        out_specs=[pl.BlockSpec(memory_space=pltpu.VMEM)] * 2,
        compiler_params=pltpu.CompilerParams(vmem_limit_bytes=20 << 20),
        cost_estimate=pl.CostEstimate(
            flops=1400000000, bytes_accessed=4 << 20, transcendentals=ROWS * SUB
        ),
        name="expect",
    )(images, volume, picked, precision)


def gather_slabs(volume, subset, projection):
    picked = pick(pick_first_kernel, "pick_first", subset, projection)
    volume, picked = lax.optimization_barrier((volume, picked))
    column = lax.all_to_all(
        jnp.broadcast_to(volume.reshape(1, 16, 128), (Z, 16, 128)), "z", 0, 0, tiled=True
    )
    picked = pick(pick_second_kernel, "pick_second", subset, projection, picked)
    column, picked = lax.optimization_barrier((column.reshape(Z, FREQ), picked))
    whole = lax.all_to_all(
        jnp.broadcast_to(column[None], (X * Y, Z, FREQ)), PLANE, 0, 0, tiled=True
    )
    return whole.reshape(SLABS, FREQ), picked


def finish_kernel(column_ref, new_ref):
    total = jnp.sum(column_ref[...].astype(F32), axis=0)
    weight = total[FREQ // 128 :, :1] + total[FREQ // 128 :, 1:2]
    new_ref[...] = total[: FREQ // 128, :] / (weight + 1.0)


def new_slab(partial):
    plane = lax.all_to_all(partial, PLANE, 0, 0, tiled=True)
    plane = jnp.sum(plane.astype(F32), axis=0).astype(BF16)
    column = lax.all_to_all(plane.reshape(Z, WIDE // 128, 128), "z", 0, 0, tiled=True)
    return pl.pallas_call(
        finish_kernel,
        out_shape=jax.ShapeDtypeStruct((FREQ // 128, 128), F32),
        in_specs=[pl.BlockSpec(memory_space=pltpu.VMEM)],
        out_specs=pl.BlockSpec(memory_space=pltpu.VMEM),
        compiler_params=pltpu.CompilerParams(vmem_limit_bytes=8 << 20),
        cost_estimate=pl.CostEstimate(flops=100000, bytes_accessed=1 << 17, transcendentals=0),
        name="finish",
    )(column).reshape(1, FREQ)


def local(images, projection, volume, subset, precision):
    gathered, picked = gather_slabs(volume, subset, projection)
    partial, evidence = expect(images, gathered, picked, precision.reshape(1, ROWS))
    return (new_slab(partial), evidence.reshape(ROWS))


def solution(mesh):
    grid = Mesh(mesh.devices.reshape(2, X, Y, Z), ("half", "x", "y", "z"))
    every = ("half", "x", "y", "z")
    placed = (P(every, None), P(), P(every, None), P(every, None), P(every))
    return jax.shard_map(
        local,
        mesh=grid,
        in_specs=placed,
        out_specs=(P(every, None), P(every)),
        check_vma=False,
    )
```

```python
import jax
import jax.numpy as jnp
from jax import lax
from jax.experimental import pallas as pl
from jax.experimental.pallas import tpu as pltpu
from jax.sharding import Mesh, PartitionSpec as P

X, Y, Z = 4, 4, 16
PLANE = ("x", "y")
SLABS, FREQ, ORI, SUB, ROWS = 256, 2048, 4096, 1024, 256
WIDE = FREQ + 128
PAIR = 1152
BF16, F32 = jnp.bfloat16, jnp.float32
NN = (((1,), (0,)), ((), ()))
NT = (((1,), (1,)), ((), ()))
TN = (((0,), (0,)), ((), ()))


def mm(a, b, dims):
    return lax.dot_general(a, b, dims, preferred_element_type=F32)


def parts(a, count):
    found = []
    for _ in range(count):
        found.append(a.astype(BF16))
        a = a - found[-1].astype(F32)
    return found


BLOCKS = 2
BLOCK = ORI // BLOCKS


def pick_rows(
    subset_hbm, projection_hbm, out_hbm, subset_ref, rows_ref, total_ref, picked_ref, sems
):
    subset_copy = pltpu.make_async_copy(subset_hbm, subset_ref, sems.at[BLOCKS])
    subset_copy.start()
    copies = []
    for b in range(BLOCKS):
        here = pl.ds(b * BLOCK, BLOCK)
        copies.append(
            pltpu.make_async_copy(projection_hbm.at[here], rows_ref.at[here], sems.at[b])
        )
        copies[-1].start()
    rows = lax.broadcasted_iota(jnp.int32, (256, SUB), 0).astype(F32).astype(BF16)
    subset_copy.wait()
    subset = subset_ref[...]
    block = subset // 256
    within = subset - block * 256
    for k in range(ORI // 256):
        wanted = jnp.where(block == k, within, -1).astype(F32).astype(BF16)
        chosen = jnp.where(rows == wanted, jnp.ones((), BF16), jnp.zeros((), BF16))
        if k * 256 % BLOCK == 0:
            copies[k * 256 // BLOCK].wait()
        part = mm(rows_ref[k * 256 : (k + 1) * 256, :], chosen, TN)
        if k == 0:
            total_ref[...] = part
        else:
            total_ref[...] += part
    picked_ref[...] = total_ref[...].astype(BF16)
    out = pltpu.make_async_copy(picked_ref, out_hbm, sems.at[BLOCKS])
    out.start()
    out.wait()


def pick_first_kernel(subset_hbm, projection_hbm, *refs):
    @pl.when(lax.axis_index("half") == 0)
    def _():
        pick_rows(subset_hbm, projection_hbm, *refs)


def pick_second_kernel(subset_hbm, projection_hbm, held_ref, *refs):
    @pl.when(lax.axis_index("half") == 1)
    def _():
        pick_rows(subset_hbm, projection_hbm, *refs)


def pick(kernel, name, subset, projection, *held):
    return pl.pallas_call(
        kernel,
        out_shape=jax.ShapeDtypeStruct((SLABS, SUB), BF16),
        in_specs=[pl.BlockSpec(memory_space=pltpu.HBM)] * (2 + len(held)),
        out_specs=pl.BlockSpec(memory_space=pltpu.HBM),
        input_output_aliases={2: 0} if held else {},
        scratch_shapes=[
            pltpu.VMEM((1, SUB), jnp.int32),
            pltpu.VMEM((ORI, SLABS), BF16),
            pltpu.VMEM((SLABS, SUB), F32),
            pltpu.VMEM((SLABS, SUB), BF16),
            pltpu.SemaphoreType.DMA((BLOCKS + 1,)),
        ],
        compiler_params=pltpu.CompilerParams(vmem_limit_bytes=60 << 20),
        cost_estimate=pl.CostEstimate(
            flops=2 * SLABS * ORI * SUB, bytes_accessed=3 << 20, transcendentals=0
        ),
        name=name,
    )(subset, projection, *held)


def expect_kernel(images_ref, volume_ref, picked_ref, precision_ref, partial_ref, evidence_ref):
    images, volume = images_ref[...], volume_ref[...]
    picked = picked_ref[...]
    gram = mm(volume, volume, NT)
    cross = mm(images, volume, NT)
    many = mm(jnp.concatenate(parts(gram, 3) + parts(cross, 3), axis=0), picked, NN)
    wide = sum(many[k * SLABS : (k + 1) * SLABS] for k in range(3))
    correlate = sum(many[k * ROWS : (k + 1) * ROWS] for k in range(3, 6))
    pfloat = picked.astype(F32)
    energy = jnp.sum(wide * pfloat, axis=0, keepdims=True)
    precision = jnp.transpose(jnp.broadcast_to(precision_ref[...], (128, ROWS)))[:, :1]
    scores = precision * (correlate - 0.5 * energy)
    highest = jnp.max(scores, axis=1, keepdims=True)
    expo = jnp.exp(scores - highest)
    summed = jnp.sum(expo, axis=1, keepdims=True)
    evidence = highest + jnp.log(summed)
    evidence_ref[...] = jnp.transpose(jnp.broadcast_to(evidence, (ROWS, 128)))[:1, :]
    weights = expo * (1.0 / summed)
    occupancy = jnp.sum(weights, axis=0, keepdims=True)
    slab_weight = jnp.sum(occupancy * (pfloat * pfloat), axis=1, keepdims=True)
    mixed = mm(picked, weights.astype(BF16), NT).astype(BF16)
    for c in range(0, FREQ, 512):
        numer = mm(mixed, images_ref[:, c : c + 512], NN)
        partial_ref[:, :, c : c + 512] = numer.astype(BF16).reshape(X * Y, Z, 512)
    lane = lax.broadcasted_iota(jnp.int32, (SLABS, 128), 1)
    high = slab_weight.astype(BF16).astype(F32)
    extra = jnp.where(lane == 0, high, jnp.where(lane == 1, slab_weight - high, 0.0))
    partial_ref[:, :, FREQ:] = extra.astype(BF16).reshape(X * Y, Z, 128)


def expect(images, volume, picked, precision):
    return pl.pallas_call(
        expect_kernel,
        out_shape=(
            jax.ShapeDtypeStruct((X * Y, Z, WIDE), BF16),
            jax.ShapeDtypeStruct((1, ROWS), F32),
        ),
        in_specs=[pl.BlockSpec(memory_space=pltpu.VMEM)] * 4,
        out_specs=[pl.BlockSpec(memory_space=pltpu.VMEM)] * 2,
        compiler_params=pltpu.CompilerParams(vmem_limit_bytes=20 << 20),
        cost_estimate=pl.CostEstimate(
            flops=1400000000, bytes_accessed=4 << 20, transcendentals=ROWS * SUB
        ),
        name="expect",
    )(images, volume, picked, precision)


def gather_slabs(volume, subset, projection):
    picked = pick(pick_first_kernel, "pick_first", subset, projection)
    volume, picked = lax.optimization_barrier((volume, picked))
    column = lax.all_to_all(
        jnp.broadcast_to(volume.reshape(1, 16, 128), (Z, 16, 128)), "z", 0, 0, tiled=True
    )
    picked = pick(pick_second_kernel, "pick_second", subset, projection, picked)
    column, picked = lax.optimization_barrier((column.reshape(Z, FREQ), picked))
    whole = lax.all_to_all(
        jnp.broadcast_to(column[None], (X * Y, Z, FREQ)), PLANE, 0, 0, tiled=True
    )
    return whole.reshape(SLABS, FREQ), picked


def finish_kernel(column_ref, new_ref):
    total = jnp.sum(column_ref[...].astype(F32), axis=0)
    lanes = [total[r : r + 1, c : c + 128] for r in range(2) for c in range(0, PAIR, 128)]
    weight = lanes[FREQ // 128][:, :1] + lanes[FREQ // 128][:, 1:2]
    new_ref[...] = jnp.concatenate(lanes[: FREQ // 128], axis=0) / (weight + 1.0)


def new_slab(partial):
    plane = lax.all_to_all(partial, PLANE, 0, 0, tiled=True)
    plane = jnp.sum(plane.astype(F32), axis=0).astype(BF16)
    plane = jnp.pad(plane, ((0, 0), (0, 2 * PAIR - WIDE))).reshape(Z, 2, PAIR)
    column = lax.all_to_all(plane, "z", 0, 0, tiled=True)
    return pl.pallas_call(
        finish_kernel,
        out_shape=jax.ShapeDtypeStruct((FREQ // 128, 128), F32),
        in_specs=[pl.BlockSpec(memory_space=pltpu.VMEM)],
        out_specs=pl.BlockSpec(memory_space=pltpu.VMEM),
        compiler_params=pltpu.CompilerParams(vmem_limit_bytes=8 << 20),
        cost_estimate=pl.CostEstimate(flops=100000, bytes_accessed=1 << 17, transcendentals=0),
        name="finish",
    )(column).reshape(1, FREQ)


def local(images, projection, volume, subset, precision):
    gathered, picked = gather_slabs(volume, subset, projection)
    partial, evidence = expect(images, gathered, picked, precision.reshape(1, ROWS))
    return (new_slab(partial), evidence.reshape(ROWS))


def solution(mesh):
    grid = Mesh(mesh.devices.reshape(2, X, Y, Z), ("half", "x", "y", "z"))
    every = ("half", "x", "y", "z")
    placed = (P(every, None), P(), P(every, None), P(every, None), P(every))
    return jax.shard_map(
        local,
        mesh=grid,
        in_specs=placed,
        out_specs=(P(every, None), P(every)),
        check_vma=False,
    )
```

```python
import jax
import jax.numpy as jnp
from jax import lax
from jax.experimental import pallas as pl
from jax.experimental.pallas import tpu as pltpu
from jax.sharding import Mesh, PartitionSpec as P

X, Y, Z = 4, 4, 16
PLANE = ("x", "y")
SLABS, FREQ, ORI, SUB, ROWS = 256, 2048, 4096, 1024, 256
WIDE = FREQ + 128
PAIR = 1152
BF16, F32 = jnp.bfloat16, jnp.float32
NN = (((1,), (0,)), ((), ()))
NT = (((1,), (1,)), ((), ()))
TN = (((0,), (0,)), ((), ()))


def mm(a, b, dims):
    return lax.dot_general(a, b, dims, preferred_element_type=F32)


def parts(a, count):
    found = []
    for _ in range(count):
        found.append(a.astype(BF16))
        a = a - found[-1].astype(F32)
    return found


BLOCKS = 4
BLOCK = ORI // BLOCKS


def pick_rows(
    subset_hbm, projection_hbm, out_hbm, subset_ref, rows_ref, total_ref, picked_ref, sems
):
    subset_copy = pltpu.make_async_copy(subset_hbm, subset_ref, sems.at[BLOCKS])
    subset_copy.start()
    copies = []
    for b in range(BLOCKS):
        here = pl.ds(b * BLOCK, BLOCK)
        copies.append(
            pltpu.make_async_copy(projection_hbm.at[here], rows_ref.at[here], sems.at[b])
        )
        copies[-1].start()
    rows = lax.broadcasted_iota(jnp.int32, (256, SUB), 0).astype(F32).astype(BF16)
    subset_copy.wait()
    subset = subset_ref[...]
    block = subset // 256
    within = subset - block * 256
    for k in range(ORI // 256):
        wanted = jnp.where(block == k, within, -1).astype(F32).astype(BF16)
        chosen = jnp.where(rows == wanted, jnp.ones((), BF16), jnp.zeros((), BF16))
        if k * 256 % BLOCK == 0:
            copies[k * 256 // BLOCK].wait()
        part = mm(rows_ref[k * 256 : (k + 1) * 256, :], chosen, TN)
        if k == 0:
            total_ref[...] = part
        else:
            total_ref[...] += part
    picked_ref[...] = total_ref[...].astype(BF16)
    out = pltpu.make_async_copy(picked_ref, out_hbm, sems.at[BLOCKS])
    out.start()
    out.wait()


def pick_first_kernel(subset_hbm, projection_hbm, *refs):
    @pl.when(lax.axis_index("half") == 0)
    def _():
        pick_rows(subset_hbm, projection_hbm, *refs)


def pick_second_kernel(subset_hbm, projection_hbm, held_ref, *refs):
    @pl.when(lax.axis_index("half") == 1)
    def _():
        pick_rows(subset_hbm, projection_hbm, *refs)


def pick(kernel, name, subset, projection, *held):
    return pl.pallas_call(
        kernel,
        out_shape=jax.ShapeDtypeStruct((SLABS, SUB), BF16),
        in_specs=[pl.BlockSpec(memory_space=pltpu.HBM)] * (2 + len(held)),
        out_specs=pl.BlockSpec(memory_space=pltpu.HBM),
        input_output_aliases={2: 0} if held else {},
        scratch_shapes=[
            pltpu.VMEM((1, SUB), jnp.int32),
            pltpu.VMEM((ORI, SLABS), BF16),
            pltpu.VMEM((SLABS, SUB), F32),
            pltpu.VMEM((SLABS, SUB), BF16),
            pltpu.SemaphoreType.DMA((BLOCKS + 1,)),
        ],
        compiler_params=pltpu.CompilerParams(vmem_limit_bytes=60 << 20),
        cost_estimate=pl.CostEstimate(
            flops=2 * SLABS * ORI * SUB, bytes_accessed=3 << 20, transcendentals=0
        ),
        name=name,
    )(subset, projection, *held)


def expect_kernel(images_ref, volume_ref, picked_ref, precision_ref, partial_ref, evidence_ref):
    images, volume = images_ref[...], volume_ref[...]
    picked = picked_ref[...]
    gram = mm(volume, volume, NT)
    cross = mm(images, volume, NT)
    many = mm(jnp.concatenate(parts(gram, 3) + parts(cross, 2), axis=0), picked, NN)
    wide = sum(many[k * SLABS : (k + 1) * SLABS] for k in range(3))
    correlate = sum(many[k * ROWS : (k + 1) * ROWS] for k in range(3, 5))
    pfloat = picked.astype(F32)
    energy = jnp.sum(wide * pfloat, axis=0, keepdims=True)
    precision = jnp.transpose(jnp.broadcast_to(precision_ref[...], (128, ROWS)))[:, :1]
    scores = precision * (correlate - 0.5 * energy)
    highest = jnp.max(scores, axis=1, keepdims=True)
    expo = jnp.exp(scores - highest)
    summed = jnp.sum(expo, axis=1, keepdims=True)
    evidence = highest + jnp.log(summed)
    evidence_ref[...] = jnp.transpose(jnp.broadcast_to(evidence, (ROWS, 128)))[:1, :]
    weights = expo * (1.0 / summed)
    occupancy = jnp.sum(weights, axis=0, keepdims=True)
    slab_weight = jnp.sum(occupancy * (pfloat * pfloat), axis=1, keepdims=True)
    mixed = mm(picked, weights.astype(BF16), NT).astype(BF16)
    for c in range(0, FREQ, 512):
        numer = mm(mixed, images_ref[:, c : c + 512], NN)
        partial_ref[:, :, c : c + 512] = numer.astype(BF16).reshape(X * Y, Z, 512)
    lane = lax.broadcasted_iota(jnp.int32, (SLABS, 128), 1)
    high = slab_weight.astype(BF16).astype(F32)
    extra = jnp.where(lane == 0, high, jnp.where(lane == 1, slab_weight - high, 0.0))
    partial_ref[:, :, FREQ:] = extra.astype(BF16).reshape(X * Y, Z, 128)


def expect(images, volume, picked, precision):
    return pl.pallas_call(
        expect_kernel,
        out_shape=(
            jax.ShapeDtypeStruct((X * Y, Z, WIDE), BF16),
            jax.ShapeDtypeStruct((1, ROWS), F32),
        ),
        in_specs=[pl.BlockSpec(memory_space=pltpu.VMEM)] * 4,
        out_specs=[pl.BlockSpec(memory_space=pltpu.VMEM)] * 2,
        compiler_params=pltpu.CompilerParams(vmem_limit_bytes=20 << 20),
        cost_estimate=pl.CostEstimate(
            flops=1400000000, bytes_accessed=4 << 20, transcendentals=ROWS * SUB
        ),
        name="expect",
    )(images, volume, picked, precision)


def spread_kernel(row_hbm, spread_hbm, row_ref, spread_ref, sem):
    come = pltpu.make_async_copy(row_hbm, row_ref, sem)
    come.start()
    come.wait()
    row = jnp.concatenate([row_ref[:, c * 128 : (c + 1) * 128] for c in range(16)], axis=0)
    for z in range(Z):
        spread_ref[z] = row
    go = pltpu.make_async_copy(spread_ref, spread_hbm, sem)
    go.start()
    go.wait()


def spread(volume):
    return pl.pallas_call(
        spread_kernel,
        out_shape=jax.ShapeDtypeStruct((Z, 16, 128), BF16),
        in_specs=[pl.BlockSpec(memory_space=pltpu.HBM)],
        out_specs=pl.BlockSpec(memory_space=pltpu.HBM),
        scratch_shapes=[
            pltpu.VMEM((1, FREQ), BF16),
            pltpu.VMEM((Z, 16, 128), BF16),
            pltpu.SemaphoreType.DMA,
        ],
        compiler_params=pltpu.CompilerParams(vmem_limit_bytes=60 << 20),
        cost_estimate=pl.CostEstimate(flops=1000, bytes_accessed=1 << 16, transcendentals=0),
        name="spread",
    )(volume)


def gather_slabs(volume, subset, projection):
    picked = pick(pick_first_kernel, "pick_first", subset, projection)
    volume, picked = lax.optimization_barrier((volume, picked))
    column = lax.all_to_all(
        spread(volume), "z", 0, 0, tiled=True
    )
    picked = pick(pick_second_kernel, "pick_second", subset, projection, picked)
    column, picked = lax.optimization_barrier((column.reshape(Z, FREQ), picked))
    whole = lax.all_to_all(
        jnp.broadcast_to(column[None], (X * Y, Z, FREQ)), PLANE, 0, 0, tiled=True
    )
    return whole.reshape(SLABS, FREQ), picked


def finish_kernel(column_ref, new_ref):
    total = jnp.sum(column_ref[...].astype(F32), axis=0)
    lanes = [total[r : r + 1, c : c + 128] for r in range(2) for c in range(0, PAIR, 128)]
    weight = lanes[FREQ // 128][:, :1] + lanes[FREQ // 128][:, 1:2]
    new_ref[...] = jnp.concatenate(lanes[: FREQ // 128], axis=0) / (weight + 1.0)


def new_slab(partial):
    plane = lax.all_to_all(partial, PLANE, 0, 0, tiled=True)
    plane = jnp.sum(plane.astype(F32), axis=0).astype(BF16)
    plane = jnp.pad(plane, ((0, 0), (0, 2 * PAIR - WIDE))).reshape(Z, 2, PAIR)
    column = lax.all_to_all(plane, "z", 0, 0, tiled=True)
    return pl.pallas_call(
        finish_kernel,
        out_shape=jax.ShapeDtypeStruct((FREQ // 128, 128), F32),
        in_specs=[pl.BlockSpec(memory_space=pltpu.VMEM)],
        out_specs=pl.BlockSpec(memory_space=pltpu.VMEM),
        compiler_params=pltpu.CompilerParams(vmem_limit_bytes=8 << 20),
        cost_estimate=pl.CostEstimate(flops=100000, bytes_accessed=1 << 17, transcendentals=0),
        name="finish",
    )(column).reshape(1, FREQ)


def local(images, projection, volume, subset, precision):
    gathered, picked = gather_slabs(volume, subset, projection)
    partial, evidence = expect(images, gathered, picked, precision.reshape(1, ROWS))
    return (new_slab(partial), evidence.reshape(ROWS))


def solution(mesh):
    grid = Mesh(mesh.devices.reshape(2, X, Y, Z), ("half", "x", "y", "z"))
    every = ("half", "x", "y", "z")
    placed = (P(every, None), P(), P(every, None), P(every, None), P(every))
    return jax.shard_map(
        local,
        mesh=grid,
        in_specs=placed,
        out_specs=(P(every, None), P(every)),
        check_vma=False,
    )
```

```python
import jax
import jax.numpy as jnp
from jax import lax
from jax.experimental import pallas as pl
from jax.experimental.pallas import tpu as pltpu
from jax.sharding import Mesh, PartitionSpec as P

X, Y, Z = 4, 4, 16
PLANE = ("x", "y")
SLABS, FREQ, ORI, SUB, ROWS = 256, 2048, 4096, 1024, 256
WIDE = FREQ + 128
PAIR = 1152
BF16, F32 = jnp.bfloat16, jnp.float32
NN = (((1,), (0,)), ((), ()))
NT = (((1,), (1,)), ((), ()))
TN = (((0,), (0,)), ((), ()))


def mm(a, b, dims):
    return lax.dot_general(a, b, dims, preferred_element_type=F32)


def parts(a, count):
    found = []
    for _ in range(count):
        found.append(a.astype(BF16))
        a = a - found[-1].astype(F32)
    return found


BLOCKS = 4
BLOCK = ORI // BLOCKS


def pick_rows(
    subset_hbm, projection_hbm, out_hbm, subset_ref, rows_ref, total_ref, picked_ref, sems
):
    subset_copy = pltpu.make_async_copy(subset_hbm, subset_ref, sems.at[BLOCKS])
    subset_copy.start()
    copies = []
    for b in range(BLOCKS):
        here = pl.ds(b * BLOCK, BLOCK)
        copies.append(
            pltpu.make_async_copy(projection_hbm.at[here], rows_ref.at[here], sems.at[b])
        )
        copies[-1].start()
    rows = lax.broadcasted_iota(jnp.int32, (256, SUB), 0).astype(F32).astype(BF16)
    subset_copy.wait()
    subset = subset_ref[...]
    block = subset // 256
    within = subset - block * 256
    for k in range(ORI // 256):
        wanted = jnp.where(block == k, within, -1).astype(F32).astype(BF16)
        chosen = jnp.where(rows == wanted, jnp.ones((), BF16), jnp.zeros((), BF16))
        if k * 256 % BLOCK == 0:
            copies[k * 256 // BLOCK].wait()
        part = mm(rows_ref[k * 256 : (k + 1) * 256, :], chosen, TN)
        if k == 0:
            total_ref[...] = part
        else:
            total_ref[...] += part
    picked_ref[...] = total_ref[...].astype(BF16)
    out = pltpu.make_async_copy(picked_ref, out_hbm, sems.at[BLOCKS])
    out.start()
    out.wait()


def pick_first_kernel(subset_hbm, projection_hbm, *refs):
    @pl.when(lax.axis_index("half") == 0)
    def _():
        pick_rows(subset_hbm, projection_hbm, *refs)


def pick_second_kernel(subset_hbm, projection_hbm, held_ref, *refs):
    @pl.when(lax.axis_index("half") == 1)
    def _():
        pick_rows(subset_hbm, projection_hbm, *refs)


def pick(kernel, name, subset, projection, *held):
    return pl.pallas_call(
        kernel,
        out_shape=jax.ShapeDtypeStruct((SLABS, SUB), BF16),
        in_specs=[pl.BlockSpec(memory_space=pltpu.HBM)] * (2 + len(held)),
        out_specs=pl.BlockSpec(memory_space=pltpu.HBM),
        input_output_aliases={2: 0} if held else {},
        scratch_shapes=[
            pltpu.VMEM((1, SUB), jnp.int32),
            pltpu.VMEM((ORI, SLABS), BF16),
            pltpu.VMEM((SLABS, SUB), F32),
            pltpu.VMEM((SLABS, SUB), BF16),
            pltpu.SemaphoreType.DMA((BLOCKS + 1,)),
        ],
        compiler_params=pltpu.CompilerParams(vmem_limit_bytes=60 << 20),
        cost_estimate=pl.CostEstimate(
            flops=2 * SLABS * ORI * SUB, bytes_accessed=3 << 20, transcendentals=0
        ),
        name=name,
    )(subset, projection, *held)


def expect_kernel(images_ref, volume_ref, picked_ref, precision_ref, partial_ref, evidence_ref):
    images, volume = images_ref[...], volume_ref[...]
    picked = picked_ref[...]
    gram = mm(volume, volume, NT)
    cross = mm(images, volume, NT)
    many = mm(jnp.concatenate(parts(gram, 3) + parts(cross, 2), axis=0), picked, NN)
    wide = sum(many[k * SLABS : (k + 1) * SLABS] for k in range(3))
    correlate = sum(many[k * ROWS : (k + 1) * ROWS] for k in range(3, 5))
    pfloat = picked.astype(F32)
    energy = jnp.sum(wide * pfloat, axis=0, keepdims=True)
    precision = jnp.transpose(jnp.broadcast_to(precision_ref[...], (128, ROWS)))[:, :1]
    occupancy, mixed, seen = 0.0, [], []
    for r in range(0, ROWS, 128):
        scores = precision[r : r + 128] * (correlate[r : r + 128] - 0.5 * energy)
        highest = jnp.max(scores, axis=1, keepdims=True)
        expo = jnp.exp(scores - highest)
        summed = jnp.sum(expo, axis=1, keepdims=True)
        seen.append(highest + jnp.log(summed))
        weights = expo * (1.0 / summed)
        occupancy += jnp.sum(weights, axis=0, keepdims=True)
        mixed.append(mm(picked, weights.astype(BF16), NT).astype(BF16))
    evidence = jnp.concatenate(seen, axis=0)
    evidence_ref[...] = jnp.transpose(jnp.broadcast_to(evidence, (ROWS, 128)))[:1, :]
    slab_weight = jnp.sum(occupancy * (pfloat * pfloat), axis=1, keepdims=True)
    mixed = jnp.concatenate(mixed, axis=1)
    for c in range(0, FREQ, 512):
        numer = mm(mixed, images_ref[:, c : c + 512], NN)
        partial_ref[:, :, c : c + 512] = numer.astype(BF16).reshape(X * Y, Z, 512)
    lane = lax.broadcasted_iota(jnp.int32, (SLABS, 128), 1)
    high = slab_weight.astype(BF16).astype(F32)
    extra = jnp.where(lane == 0, high, jnp.where(lane == 1, slab_weight - high, 0.0))
    partial_ref[:, :, FREQ:] = extra.astype(BF16).reshape(X * Y, Z, 128)


def expect(images, volume, picked, precision):
    return pl.pallas_call(
        expect_kernel,
        out_shape=(
            jax.ShapeDtypeStruct((X * Y, Z, WIDE), BF16),
            jax.ShapeDtypeStruct((1, ROWS), F32),
        ),
        in_specs=[pl.BlockSpec(memory_space=pltpu.VMEM)] * 4,
        out_specs=[pl.BlockSpec(memory_space=pltpu.VMEM)] * 2,
        compiler_params=pltpu.CompilerParams(vmem_limit_bytes=20 << 20),
        cost_estimate=pl.CostEstimate(
            flops=1400000000, bytes_accessed=4 << 20, transcendentals=ROWS * SUB
        ),
        name="expect",
    )(images, volume, picked, precision)


def spread_kernel(row_hbm, spread_hbm, row_ref, spread_ref, sem):
    come = pltpu.make_async_copy(row_hbm, row_ref, sem)
    come.start()
    come.wait()
    row = jnp.concatenate([row_ref[:, c * 128 : (c + 1) * 128] for c in range(16)], axis=0)
    for z in range(Z):
        spread_ref[z] = row
    go = pltpu.make_async_copy(spread_ref, spread_hbm, sem)
    go.start()
    go.wait()


def spread(volume):
    return pl.pallas_call(
        spread_kernel,
        out_shape=jax.ShapeDtypeStruct((Z, 16, 128), BF16),
        in_specs=[pl.BlockSpec(memory_space=pltpu.HBM)],
        out_specs=pl.BlockSpec(memory_space=pltpu.HBM),
        scratch_shapes=[
            pltpu.VMEM((1, FREQ), BF16),
            pltpu.VMEM((Z, 16, 128), BF16),
            pltpu.SemaphoreType.DMA,
        ],
        compiler_params=pltpu.CompilerParams(vmem_limit_bytes=60 << 20),
        cost_estimate=pl.CostEstimate(flops=1000, bytes_accessed=1 << 16, transcendentals=0),
        name="spread",
    )(volume)


def gather_slabs(volume, subset, projection):
    picked = pick(pick_first_kernel, "pick_first", subset, projection)
    volume, picked = lax.optimization_barrier((volume, picked))
    column = lax.all_to_all(
        spread(volume), "z", 0, 0, tiled=True
    )
    picked = pick(pick_second_kernel, "pick_second", subset, projection, picked)
    column, picked = lax.optimization_barrier((column.reshape(Z, FREQ), picked))
    whole = lax.all_to_all(
        jnp.broadcast_to(column[None], (X * Y, Z, FREQ)), PLANE, 0, 0, tiled=True
    )
    return whole.reshape(SLABS, FREQ), picked


def finish_kernel(column_ref, new_ref):
    total = jnp.sum(column_ref[...].astype(F32), axis=0)
    lanes = [total[r : r + 1, c : c + 128] for r in range(2) for c in range(0, PAIR, 128)]
    weight = lanes[FREQ // 128][:, :1] + lanes[FREQ // 128][:, 1:2]
    new_ref[...] = jnp.concatenate(lanes[: FREQ // 128], axis=0) / (weight + 1.0)


def new_slab(partial):
    plane = lax.all_to_all(partial, PLANE, 0, 0, tiled=True)
    plane = jnp.sum(plane.astype(F32), axis=0).astype(BF16)
    plane = jnp.pad(plane, ((0, 0), (0, 2 * PAIR - WIDE))).reshape(Z, 2, PAIR)
    column = lax.all_to_all(plane, "z", 0, 0, tiled=True)
    return pl.pallas_call(
        finish_kernel,
        out_shape=jax.ShapeDtypeStruct((FREQ // 128, 128), F32),
        in_specs=[pl.BlockSpec(memory_space=pltpu.VMEM)],
        out_specs=pl.BlockSpec(memory_space=pltpu.VMEM),
        compiler_params=pltpu.CompilerParams(vmem_limit_bytes=8 << 20),
        cost_estimate=pl.CostEstimate(flops=100000, bytes_accessed=1 << 17, transcendentals=0),
        name="finish",
    )(column).reshape(1, FREQ)


def local(images, projection, volume, subset, precision):
    gathered, picked = gather_slabs(volume, subset, projection)
    partial, evidence = expect(images, gathered, picked, precision.reshape(1, ROWS))
    return (new_slab(partial), evidence.reshape(ROWS))


def solution(mesh):
    grid = Mesh(mesh.devices.reshape(2, X, Y, Z), ("half", "x", "y", "z"))
    every = ("half", "x", "y", "z")
    placed = (P(every, None), P(), P(every, None), P(every, None), P(every))
    return jax.shard_map(
        local,
        mesh=grid,
        in_specs=placed,
        out_specs=(P(every, None), P(every)),
        check_vma=False,
    )
```

```python
import jax
import jax.numpy as jnp
from jax import lax
from jax.experimental import pallas as pl
from jax.experimental.pallas import tpu as pltpu
from jax.sharding import Mesh, PartitionSpec as P

X, Y, Z = 4, 4, 16
PLANE = ("x", "y")
SLABS, FREQ, ORI, SUB, ROWS = 256, 2048, 4096, 1024, 256
WIDE = FREQ + 128
PAIR = 1152
BF16, F32 = jnp.bfloat16, jnp.float32
NN = (((1,), (0,)), ((), ()))
NT = (((1,), (1,)), ((), ()))
TN = (((0,), (0,)), ((), ()))


def mm(a, b, dims):
    return lax.dot_general(a, b, dims, preferred_element_type=F32)


def parts(a, count):
    found = []
    for _ in range(count):
        found.append(a.astype(BF16))
        a = a - found[-1].astype(F32)
    return found


BLOCKS = 2
BLOCK = ORI // BLOCKS


def pick_rows(
    subset_hbm, projection_hbm, out_hbm, subset_ref, rows_ref, total_ref, picked_ref, sems
):
    subset_copy = pltpu.make_async_copy(subset_hbm, subset_ref, sems.at[BLOCKS])
    subset_copy.start()
    copies = []
    for b in range(BLOCKS):
        here = pl.ds(b * BLOCK, BLOCK)
        copies.append(
            pltpu.make_async_copy(projection_hbm.at[here], rows_ref.at[here], sems.at[b])
        )
        copies[-1].start()
    rows = lax.broadcasted_iota(jnp.int32, (256, SUB), 0).astype(F32).astype(BF16)
    subset_copy.wait()
    subset = subset_ref[...]
    block = subset // 256
    within = subset - block * 256
    for k in range(ORI // 256):
        wanted = jnp.where(block == k, within, -1).astype(F32).astype(BF16)
        chosen = jnp.where(rows == wanted, jnp.ones((), BF16), jnp.zeros((), BF16))
        if k * 256 % BLOCK == 0:
            copies[k * 256 // BLOCK].wait()
        part = mm(rows_ref[k * 256 : (k + 1) * 256, :], chosen, TN)
        if k == 0:
            total_ref[...] = part
        else:
            total_ref[...] += part
    picked_ref[...] = total_ref[...].astype(BF16)
    out = pltpu.make_async_copy(picked_ref, out_hbm, sems.at[BLOCKS])
    out.start()
    out.wait()


def pick_first_kernel(
    subset_hbm, projection_hbm, row_hbm, picked_hbm, spread_hbm, row_ref, spread_ref, row_sem, *scratch
):
    come = pltpu.make_async_copy(row_hbm, row_ref, row_sem)
    go = pltpu.make_async_copy(spread_ref, spread_hbm, row_sem)
    come.start()
    come.wait()
    row = jnp.concatenate([row_ref[:, c * 128 : (c + 1) * 128] for c in range(16)], axis=0)
    for z in range(Z):
        spread_ref[z] = row
    go.start()

    @pl.when(lax.axis_index("half") == 0)
    def _():
        pick_rows(subset_hbm, projection_hbm, picked_hbm, *scratch)

    go.wait()


def pick_second_kernel(subset_hbm, projection_hbm, held_hbm, picked_hbm, *scratch):
    @pl.when(lax.axis_index("half") == 1)
    def _():
        pick_rows(subset_hbm, projection_hbm, picked_hbm, *scratch)


PICKED = jax.ShapeDtypeStruct((SLABS, SUB), BF16)
SCRATCH = [
    pltpu.VMEM((1, SUB), jnp.int32),
    pltpu.VMEM((ORI, SLABS), BF16),
    pltpu.VMEM((SLABS, SUB), F32),
    pltpu.VMEM((SLABS, SUB), BF16),
    pltpu.SemaphoreType.DMA((BLOCKS + 1,)),
]
PICK_PARAMS = dict(
    compiler_params=pltpu.CompilerParams(vmem_limit_bytes=60 << 20),
    cost_estimate=pl.CostEstimate(
        flops=2 * SLABS * ORI * SUB, bytes_accessed=3 << 20, transcendentals=0
    ),
)


def pick_first(subset, projection, row):
    return pl.pallas_call(
        pick_first_kernel,
        out_shape=(PICKED, jax.ShapeDtypeStruct((Z, 16, 128), BF16)),
        in_specs=[pl.BlockSpec(memory_space=pltpu.HBM)] * 3,
        out_specs=[pl.BlockSpec(memory_space=pltpu.HBM)] * 2,
        scratch_shapes=[
            pltpu.VMEM((1, FREQ), BF16),
            pltpu.VMEM((Z, 16, 128), BF16),
            pltpu.SemaphoreType.DMA,
        ]
        + SCRATCH,
        name="pick_first",
        **PICK_PARAMS,
    )(subset, projection, row)


def pick_second(subset, projection, held):
    return pl.pallas_call(
        pick_second_kernel,
        out_shape=PICKED,
        in_specs=[pl.BlockSpec(memory_space=pltpu.HBM)] * 3,
        out_specs=pl.BlockSpec(memory_space=pltpu.HBM),
        input_output_aliases={2: 0},
        scratch_shapes=SCRATCH,
        name="pick_second",
        **PICK_PARAMS,
    )(subset, projection, held)


def expect_kernel(images_ref, volume_ref, picked_ref, precision_ref, partial_ref, evidence_ref):
    images, volume = images_ref[...], volume_ref[...]
    picked = picked_ref[...]
    gram = mm(volume, volume, NT)
    cross = mm(images, volume, NT)
    many = mm(jnp.concatenate(parts(gram, 3) + parts(cross, 2), axis=0), picked, NN)
    wide = sum(many[k * SLABS : (k + 1) * SLABS] for k in range(3))
    correlate = sum(many[k * ROWS : (k + 1) * ROWS] for k in range(3, 5))
    pfloat = picked.astype(F32)
    energy = jnp.sum(wide * pfloat, axis=0, keepdims=True)
    precision = jnp.transpose(jnp.broadcast_to(precision_ref[...], (128, ROWS)))[:, :1]
    occupancy, mixed, seen = 0.0, [], []
    for r in range(0, ROWS, 128):
        scores = precision[r : r + 128] * (correlate[r : r + 128] - 0.5 * energy)
        highest = jnp.max(scores, axis=1, keepdims=True)
        expo = jnp.exp(scores - highest)
        summed = jnp.sum(expo, axis=1, keepdims=True)
        seen.append(highest + jnp.log(summed))
        weights = expo * (1.0 / summed)
        occupancy += jnp.sum(weights, axis=0, keepdims=True)
        mixed.append(mm(picked, weights.astype(BF16), NT).astype(BF16))
    evidence = jnp.concatenate(seen, axis=0)
    evidence_ref[...] = jnp.transpose(jnp.broadcast_to(evidence, (ROWS, 128)))[:1, :]
    slab_weight = jnp.sum(occupancy * (pfloat * pfloat), axis=1, keepdims=True)
    mixed = jnp.concatenate(mixed, axis=1)
    for c in range(0, FREQ, 512):
        numer = mm(mixed, images_ref[:, c : c + 512], NN)
        partial_ref[:, :, c : c + 512] = numer.astype(BF16).reshape(X * Y, Z, 512)
    lane = lax.broadcasted_iota(jnp.int32, (SLABS, 128), 1)
    high = slab_weight.astype(BF16).astype(F32)
    extra = jnp.where(lane == 0, high, jnp.where(lane == 1, slab_weight - high, 0.0))
    partial_ref[:, :, FREQ:] = extra.astype(BF16).reshape(X * Y, Z, 128)


def expect(images, volume, picked, precision):
    return pl.pallas_call(
        expect_kernel,
        out_shape=(
            jax.ShapeDtypeStruct((X * Y, Z, WIDE), BF16),
            jax.ShapeDtypeStruct((1, ROWS), F32),
        ),
        in_specs=[pl.BlockSpec(memory_space=pltpu.VMEM)] * 4,
        out_specs=[pl.BlockSpec(memory_space=pltpu.VMEM)] * 2,
        compiler_params=pltpu.CompilerParams(vmem_limit_bytes=20 << 20),
        cost_estimate=pl.CostEstimate(
            flops=1400000000, bytes_accessed=4 << 20, transcendentals=ROWS * SUB
        ),
        name="expect",
    )(images, volume, picked, precision)


def gather_slabs(volume, subset, projection):
    picked, rows = pick_first(subset, projection, volume)
    column = lax.all_to_all(rows, "z", 0, 0, tiled=True)
    picked = pick_second(subset, projection, picked)
    column, picked = lax.optimization_barrier((column.reshape(Z, FREQ), picked))
    whole = lax.all_to_all(
        jnp.broadcast_to(column[None], (X * Y, Z, FREQ)), PLANE, 0, 0, tiled=True
    )
    return whole.reshape(SLABS, FREQ), picked


def finish_kernel(column_ref, new_ref):
    total = jnp.sum(column_ref[...].astype(F32), axis=0)
    lanes = [total[r : r + 1, c : c + 128] for r in range(2) for c in range(0, PAIR, 128)]
    weight = lanes[FREQ // 128][:, :1] + lanes[FREQ // 128][:, 1:2]
    new_ref[...] = jnp.concatenate(lanes[: FREQ // 128], axis=0) / (weight + 1.0)


def new_slab(partial):
    plane = lax.all_to_all(partial, PLANE, 0, 0, tiled=True)
    plane = jnp.sum(plane.astype(F32), axis=0).astype(BF16)
    plane = jnp.pad(plane, ((0, 0), (0, 2 * PAIR - WIDE))).reshape(Z, 2, PAIR)
    column = lax.all_to_all(plane, "z", 0, 0, tiled=True)
    return pl.pallas_call(
        finish_kernel,
        out_shape=jax.ShapeDtypeStruct((FREQ // 128, 128), F32),
        in_specs=[pl.BlockSpec(memory_space=pltpu.VMEM)],
        out_specs=pl.BlockSpec(memory_space=pltpu.VMEM),
        compiler_params=pltpu.CompilerParams(vmem_limit_bytes=8 << 20),
        cost_estimate=pl.CostEstimate(flops=100000, bytes_accessed=1 << 17, transcendentals=0),
        name="finish",
    )(column).reshape(1, FREQ)


def local(images, projection, volume, subset, precision):
    gathered, picked = gather_slabs(volume, subset, projection)
    partial, evidence = expect(images, gathered, picked, precision.reshape(1, ROWS))
    return (new_slab(partial), evidence.reshape(ROWS))


def solution(mesh):
    grid = Mesh(mesh.devices.reshape(2, X, Y, Z), ("half", "x", "y", "z"))
    every = ("half", "x", "y", "z")
    placed = (P(every, None), P(), P(every, None), P(every, None), P(every))
    return jax.shard_map(
        local,
        mesh=grid,
        in_specs=placed,
        out_specs=(P(every, None), P(every)),
        check_vma=False,
    )
```
